512 devices in a mesh: pool: 4 (over z_hi, core), dp: 16 (over y, x), head: 8 (over z_lo).
Axes of the slice: x: 4, y: 4, z: 16 (z_hi: 2, z_lo: 8; z = z_hi * 8 + z_lo), core: 2. Of those that a mesh axis runs over, the one named last changes fastest.
Arguments:
- queries: bfloat16 [256, 8192], P(('pool', 'dp'), 'head'), may hold values from -240 to 240
- fresh_kv: bfloat16 [2, 256, 1024], P(None, ('pool', 'dp'), 'head'), may hold values from -6 to 6
- key_value_pages: bfloat16 [2, 1536, 64, 1024], P(None, ('pool', 'dp'), None, 'head'), may hold values from -6 to 6
- page_table: int32 [256, 8], P(('pool', 'dp')), may hold values from 0 to 23, as said below
- lengths: int32 [256], P(('pool', 'dp')), may hold values from 1 to 512, as said below
- cache_scales: float32 [2, 8], P(None, 'head'), may hold values from 0.5 to 2
- residual: bfloat16 [256, 8192], P(('pool', 'head'), 'dp'), may hold values from -13 to 13
- out_weight: bfloat16 [8192, 8192], P('head', 'dp'), may hold values from -0.0625 to 0.0625
- norm_gain: float32 [8192], P('dp'), may hold values from 0.25 to 1.75
- gate_up: bfloat16 [2, 8192, 24576], P(None, 'dp', ('pool', 'head')), may hold values from -0.0625 to 0.0625
- down_weight: bfloat16 [24576, 8192], P(('pool', 'head'), 'dp'), may hold values from -0.0390625 to 0.0390625
Outputs:
- layer_out: bfloat16 [256, 8192], P(('pool', 'head'), 'dp')
The draws below stay inside these ranges and needn't reach their ends.
Inputs may be any that keep to these rules, and one draw needn't show every extreme that they name: `lengths`: in each aligned block of 4 requests (one block of pages), exactly one length equals 512; every other length is at most 256. `page_table`: entries number the 24 pages of the request's own block. Over the requests of one block, the first ceil(length / 64) entries of each request are all distinct; later entries are any pages and are not read.
All inputs are finite; a program needn't handle non-finite values.
Results may differ from the reference program's by a relative error of at most 0.024.
Values may be sent and summed in bfloat16 or wider, within the bound.
A program may use at most 64 MiB of HBM per device.

```python
import math
import jax
import jax.numpy as jnp
from jax import lax

D = 8192
QHEADS = 64
KVHEADS = 8
HEAD_DIM = 128
FF = 24576
B_DEV = 4
CTX = 512
PAGE = 64
PPR = 8
NPAGE = 24
TOKENS = 256
N_DP = 16


def page_plan(key):
    blocks = TOKENS // B_DEV
    cap_key, len_key, top_key, perm_key = jax.random.split(key, 4)
    caps = jax.random.randint(cap_key, (blocks, 1), CTX // 8, CTX // 2 + 1)
    raw = jax.random.randint(len_key, (blocks, B_DEV), 0, 1 << 20)
    sizes = 1 + raw % caps
    longest = jax.random.randint(top_key, (blocks, 1), 0, B_DEV)
    sizes = jnp.where(jnp.arange(B_DEV, dtype=jnp.int32)[None, :] == longest, CTX, sizes)
    used = (sizes + PAGE - 1) // PAGE
    first = jnp.cumsum(used, axis=1) - used
    orders = jax.vmap(lambda k: jax.random.permutation(k, NPAGE))(jax.random.split(perm_key, blocks))
    slots = (first[:, :, None] + jnp.arange(PPR, dtype=jnp.int32)[None, None, :]) % NPAGE
    table = jnp.take_along_axis(orders, slots.reshape(blocks, B_DEV * PPR), axis=1)
    return (sizes.reshape(TOKENS).astype(jnp.int32), table.reshape(TOKENS, PPR).astype(jnp.int32))


def draw_lengths(key, part):
    sizes, table = page_plan(key)
    return sizes


def draw_page_table(key, part):
    sizes, table = page_plan(key)
    return table


def draw_queries(key, part):
    key = jax.random.fold_in(key, 5)
    base = jax.random.normal(key, (TOKENS, QHEADS, HEAD_DIM), jnp.float32)
    return jnp.clip(base, -240.0, 240.0).reshape(TOKENS, QHEADS * HEAD_DIM).astype(jnp.bfloat16)


def draw_residual(key, part):
    key = jax.random.fold_in(key, 7)
    columns = jnp.arange(D, dtype=jnp.float32) / (D - 1)
    rough = jnp.exp(jax.random.uniform(jax.random.fold_in(key, 1), (D,), jnp.float32, math.log(0.7), math.log(1.4)))
    scale = jnp.exp(math.log(3.0) * columns) * rough
    values = 0.5 * jax.random.normal(key, (TOKENS, D), jnp.float32) * scale[None, :]
    return jnp.clip(values, -13.0, 13.0).astype(jnp.bfloat16)


def shard_levels(stream_key, dims, pieces, smallest, top_value):
    loudness, own = 1.0, jax.random.fold_in(stream_key, 6)
    for dim, shards_of in pieces:
        heights = jnp.exp(jax.random.uniform(jax.random.fold_in(own, dim), (shards_of,), jnp.float32, smallest / len(pieces), top_value / len(pieces)))
        loudness = loudness * jnp.repeat(heights, dims[dim] // shards_of).reshape([-1 if axis == dim else 1 for axis in range(len(dims))])
    return loudness


def centred(key, shape, width, bound, cuts=(), held_as=jnp.bfloat16):
    entries = jax.random.normal(key, shape, jnp.float32) * width
    if len(cuts) > 0:
        entries = shard_levels(key, shape, cuts, -0.22, 0.18) * entries
    return jnp.clip(entries, min=-bound, max=bound).astype(held_as)


def setup_inputs(seed: int = 0) -> dict:
    arg_keys = jax.random.split(jax.random.key(seed), 12)
    return {
        "queries": draw_queries(jax.random.fold_in(arg_keys[11], 71), 0),
        "fresh_kv": centred(arg_keys[1], (2, TOKENS, KVHEADS * HEAD_DIM), 1.0, 6.0, ((1, 64), (2, 8))),
        "key_value_pages": centred(arg_keys[2], (2, TOKENS // B_DEV * NPAGE, PAGE, KVHEADS * HEAD_DIM), 1.0, 6.0, ((1, 64), (3, 8))),
        "page_table": draw_page_table(jax.random.fold_in(arg_keys[11], 71), 0),
        "lengths": draw_lengths(jax.random.fold_in(arg_keys[11], 71), 0),
        "cache_scales": jnp.clip(jnp.exp(math.log(2.0) - 1.3862944 * jax.random.uniform(arg_keys[5], (2, KVHEADS), jnp.float32) ** shard_levels(arg_keys[5], (2, KVHEADS), ((1, 8),), -0.2, 0.2)), 0.5, 2.0),
        "residual": draw_residual(jax.random.fold_in(arg_keys[11], 71), 0),
        "out_weight": centred(arg_keys[7], (QHEADS * HEAD_DIM, D), (QHEADS * HEAD_DIM) ** -0.5, 0.0625, ((0, 8), (1, 16))),
        "norm_gain": jnp.clip(1.0 + 0.15 * jax.random.normal(arg_keys[8], (D,), jnp.float32), 0.25, 1.75),
        "gate_up": centred(arg_keys[9], (2, D, FF), D ** -0.5, 0.0625, ((1, 16), (2, 32))),
        "down_weight": centred(arg_keys[10], (FF, D), FF ** -0.5, 0.0390625, ((0, 32), (1, 16))),
    }


def attend(queries, fresh_kv, pages, table, lengths, scales):
    rows = queries.shape[0]
    heads = scales.shape[1]
    group = queries.shape[1] // (heads * HEAD_DIM)
    span = table.shape[1] * pages.shape[2]
    keys = pages[0][table].reshape(rows, span, heads, HEAD_DIM).astype(jnp.float32)
    values = pages[1][table].reshape(rows, span, heads, HEAD_DIM).astype(jnp.float32)
    asked = queries.reshape(rows, heads, group, HEAD_DIM).astype(jnp.float32)
    fresh_keys = fresh_kv[0].reshape(rows, heads, HEAD_DIM).astype(jnp.float32)
    fresh_values = fresh_kv[1].reshape(rows, heads, HEAD_DIM).astype(jnp.float32)
    factor = 1.0 / math.sqrt(HEAD_DIM)
    scores = jnp.einsum('bhgd,bshd->bhgs', asked, keys) * (scales[0] * factor)[None, :, None, None]
    own = jnp.einsum('bhgd,bhd->bhg', asked, fresh_keys) * factor
    live = jnp.arange(span, dtype=jnp.int32)[None, None, None, :] < lengths[:, None, None, None]
    top = jnp.maximum(lax.optimization_barrier(jnp.max(jnp.where(live, scores, -jnp.inf), axis=3)), own)
    weights = jnp.where(live, jnp.exp(scores - top[..., None]), 0.0)
    own_weight = jnp.exp(own - top)
    total = lax.optimization_barrier(jnp.sum(weights, axis=3)) + own_weight
    probs = (weights / total[..., None]).astype(jnp.bfloat16).astype(jnp.float32)
    own_prob = (own_weight / total).astype(jnp.bfloat16).astype(jnp.float32)
    mixed = jnp.einsum('bhgs,bshd->bhgd', probs, values) * scales[1][None, :, None, None]
    mixed = mixed + own_prob[..., None] * fresh_values[:, :, None, :]
    return mixed.reshape(rows, heads * group * HEAD_DIM).astype(jnp.bfloat16)

def reference(queries, fresh_kv, key_value_pages, page_table, lengths, cache_scales, residual, out_weight, norm_gain, gate_up, down_weight):
    blocks = TOKENS // B_DEV

    def one_block(index):
        start = index * B_DEV
        return attend(lax.dynamic_slice_in_dim(queries, start, B_DEV, 0), lax.dynamic_slice_in_dim(fresh_kv, start, B_DEV, 1), lax.dynamic_slice_in_dim(key_value_pages, index * NPAGE, NPAGE, 1), lax.dynamic_slice_in_dim(page_table, start, B_DEV, 0), lax.dynamic_slice_in_dim(lengths, start, B_DEV, 0), cache_scales)
    attended = lax.map(one_block, jnp.arange(blocks, dtype=jnp.int32)).reshape(TOKENS, QHEADS * HEAD_DIM)
    stream = residual.astype(jnp.float32) + jnp.dot(attended, out_weight, preferred_element_type=jnp.float32)
    mean_square = lax.optimization_barrier(jnp.mean(stream * stream, axis=1))
    normed = (stream * lax.rsqrt(mean_square + 1e-06)[:, None] * norm_gain[None, :]).astype(jnp.bfloat16)
    width_block = D // N_DP

    def add_block(carry, index):
        start = index * width_block
        piece = lax.dynamic_slice_in_dim(normed, start, width_block, 1)
        gate_part = jnp.dot(piece, lax.dynamic_slice_in_dim(gate_up[0], start, width_block, 0), preferred_element_type=jnp.float32)
        up_part = jnp.dot(piece, lax.dynamic_slice_in_dim(gate_up[1], start, width_block, 0), preferred_element_type=jnp.float32)
        gate_part, up_part = lax.optimization_barrier((gate_part.astype(jnp.bfloat16), up_part.astype(jnp.bfloat16)))
        return ((carry[0] + gate_part.astype(jnp.float32), carry[1] + up_part.astype(jnp.float32)), None)
    empty = jnp.zeros((TOKENS, FF), jnp.float32)
    (gate, up), unused = lax.scan(add_block, (empty, empty), jnp.arange(N_DP, dtype=jnp.int32))
    hidden = (jax.nn.silu(gate) * up).astype(jnp.bfloat16)
    lowered = jnp.dot(hidden, down_weight, preferred_element_type=jnp.float32)
    return (stream + lowered).astype(jnp.bfloat16)
```

```python
import math

import jax
import jax.numpy as jnp
from jax import lax
from jax.experimental import pallas as pl
from jax.experimental.pallas import tpu as pltpu
from jax.sharding import PartitionSpec as P

D = 8192
HEAD_DIM = 128
MESH = pl.DeviceIdType.MESH
F32 = jnp.float32
BF16 = jnp.bfloat16


def place():
    pool, dp, head = (lax.axis_index(name) for name in ("pool", "dp", "head"))
    return (pool // 2) * 8 + head, pool % 2, dp // 4, dp % 4


def device(z, core, y, x):
    return ((z // 8) * 2 + core, y * 4 + x, z % 8)


def send(src, dst, send_sem, recv_sem, to):
    pltpu.make_async_remote_copy(
        src_ref=src, dst_ref=dst, send_sem=send_sem, recv_sem=recv_sem,
        device_id=to, device_id_type=MESH,
    ).start()


def wait(ref, sem):
    pltpu.make_async_copy(ref, ref, sem).wait()


def to_tile(v):
    return jnp.concatenate([v[..., :256], v[..., 256:]], axis=-2).astype(BF16)


def from_tile(v):
    v = v.astype(F32)
    return jnp.concatenate([v[..., :8, :], v[..., 8:, :]], axis=-1)


def attend(q_ref, fresh_ref, kv, table, lengths, scales, q_rows, fresh_rows):
    q = q_ref[...].astype(F32)
    for g in range(8):
        q_rows[g * 4 : g * 4 + 4, :] = q[:, g * 128 : (g + 1) * 128]
    fresh = fresh_ref[...].astype(F32)
    for i in range(2):
        fresh_rows[i, 0:4, :] = fresh[i]
        fresh_rows[i, 4:8, :] = fresh[i]
    asked = q_rows[...]
    row = lax.broadcasted_iota(jnp.int32, (8, 1), 0) & 3
    column = lax.broadcasted_iota(jnp.int32, (8, 1536), 1)
    page, line = column >> 6, column & 63

    def by_request(values):
        a, b, c, d = values
        return jnp.where(row == 0, a, jnp.where(row == 1, b, jnp.where(row == 2, c, d)))

    length = by_request([lengths[t] for t in range(4)])
    live = jnp.zeros((8, 1536), jnp.bool_)
    for j in range(8):
        entry = by_request([table[t, j] for t in range(4)])
        live = live | ((page == entry) & (line < length - 64 * j))
    factor = 1.0 / math.sqrt(HEAD_DIM)
    keys = kv[0].reshape(1536, 128)
    scores = lax.dot_general(
        asked.astype(BF16), keys, (((1,), (1,)), ((), ())), preferred_element_type=F32
    ) * (scales[0, 0] * factor)
    scores = jnp.where(live[None], scores.reshape(4, 8, 1536), -jnp.inf)
    own = jnp.sum(asked.reshape(4, 8, 128) * fresh_rows[0][None], axis=2, keepdims=True) * factor
    top = jnp.maximum(jnp.max(scores, axis=2, keepdims=True), own)
    e = jnp.exp(scores - top)
    e_own = jnp.exp(own - top)
    total = jnp.sum(e, axis=2, keepdims=True) + e_own
    probs = (e / total).astype(BF16)
    own_prob = (e_own / total).astype(BF16).astype(F32)
    mixed = jnp.dot(
        probs.reshape(32, 1536), kv[1].reshape(1536, 128), preferred_element_type=F32
    ) * scales[1, 0]
    mixed = mixed.reshape(4, 8, 128) + own_prob * fresh_rows[1][None]
    return mixed.reshape(32, 128).astype(BF16)


def kernel(
    q_ref, fresh_ref, pages_hbm, table, lengths, scales, residual_ref, out_w_hbm, gain_ref,
    gate_up_hbm, down_hbm, out_ref,
    kv, out_w, gate_up, down, q_rows, fresh_rows, att, b_send, b_recv, stream, normed,
    d_send, d_recv, sq_part, sq_send, sq_recv, hidden, g_own, sib_send, sib_recv,
    g1_send, g1_recv, g1_own, g2_send, g2_recv,
    load_sem, a_sem, b_sem, c_sem, d_sem, sq_sem, h_sem, sib_sem, g1_sem, g2_sem,
):
    z, core, y, x = place()
    dp = y * 4 + x
    head = z % 8
    cls, block = z % 4, z // 4

    loads = []
    for i, (src, dst) in enumerate(
        ((pages_hbm, kv), (out_w_hbm, out_w), (gate_up_hbm, gate_up), (down_hbm, down))
    ):
        loads.append(pltpu.make_async_copy(src, dst, load_sem.at[i]))
        loads[-1].start()

    def plane(k):
        return device(z, core, (y + k // 4) % 4, (x + k % 4) % 4)

    def line(k):
        return device((z // 8) * 8 + (head + k) % 8, core, y, x)

    def ring(k):
        return device((z + k + 16) % 16, core, y, x)

    sibling = device(z, 1 - core, y, x)

    barrier = pltpu.get_barrier_semaphore()

    def greet(to):
        pl.semaphore_signal(barrier, inc=1, device_id=to, device_id_type=MESH)

    for k in range(1, 16):
        greet(plane(k))
    for k in range(1, 8):
        greet(line(k))
    for k in (1, -1, 2, -2, 4, -4, 8):
        greet(ring(k))
    greet(sibling)

    loads[0].wait()
    att[dp] = attend(q_ref, fresh_ref, kv, table, lengths, scales, q_rows, fresh_rows)
    pl.semaphore_wait(barrier, 30)
    for k in range(1, 16):
        send(att.at[dp], att.at[dp], a_sem.at[0], a_sem.at[1], plane(k))
    loads[1].wait()
    wait(att.at[0:15], a_sem.at[1])

    rows = att[...].astype(F32).reshape(8, 2, 4, 8, 128)
    even, odd = rows[:, 0], rows[:, 1]
    upper = lax.broadcasted_iota(jnp.int32, (8, 128), 0) < 4

    def swap(v):
        return pltpu.roll(v.reshape(32 * 8, 128).reshape(32, 8, 128), 4, 1).reshape(8, 4, 8, 128)

    low = jnp.where(upper, even, swap(odd))
    high = jnp.where(upper, swap(even), odd)
    columns = []
    for g in range(8):
        columns.append((low if g % 2 == 0 else high)[:, g // 2].reshape(64, 128))
    attended = jnp.concatenate(columns, axis=1).astype(BF16)
    projected = jnp.dot(attended, out_w[...], preferred_element_type=F32)
    b_send[...] = to_tile(projected.reshape(8, 8, 512))
    for k in range(1, 8):
        send(b_send.at[(head + k) % 8], b_recv.at[head], b_sem.at[0], b_sem.at[1], line(k))
    b_recv[head] = b_send[head]
    wait(b_recv.at[0:7], b_sem.at[1])
    summed = from_tile(jnp.sum(b_recv[...].astype(F32), axis=0))
    stream[...] = residual_ref[...].astype(F32) + summed

    gain = gain_ref[...].reshape(1, 512)
    normed[core, cls, block] = to_tile(stream[...] * gain)
    mine = normed.at[core, cls, block]
    for k in (1, 2, 3):
        send(mine, mine, c_sem.at[0], c_sem.at[1], ring(4 * k))
    wait(normed.at[0, 0, 0:3], c_sem.at[1])
    whole = normed.at[core, cls]
    send(whole, whole, c_sem.at[2], c_sem.at[3], ring(1))
    send(whole, whole, c_sem.at[2], c_sem.at[4], ring(-1))
    for i, k in ((0, 2), (1, -2)):
        half = normed.at[core, cls, 2 * i : 2 * i + 2]
        send(half, half, c_sem.at[2], c_sem.at[5], ring(k))
    send(whole, whole, c_sem.at[6], c_sem.at[7], sibling)

    inverse = 1.0 / (gain * gain)

    def feed(half, c):
        tokens = from_tile(normed[half, c]).reshape(32, 512)
        squares = tokens * tokens * inverse
        sq_part[half, c] = (
            squares[:, :128] + squares[:, 128:256] + squares[:, 256:384] + squares[:, 384:]
        ).reshape(4, 8, 128)
        lhs = tokens.astype(BF16)
        gate = jnp.dot(lhs, gate_up[0], preferred_element_type=F32).reshape(4, 8, 768)
        up = jnp.dot(lhs, gate_up[1], preferred_element_type=F32).reshape(4, 8, 768)
        d_send[half, c] = jnp.concatenate([gate, up], axis=1).astype(BF16)
        for a in range(4):
            oy, ox = a, (c + a) % 4
            same = (oy == y) & (ox == x)

            @pl.when(jnp.logical_not(same))
            def _():
                send(
                    d_send.at[half, c, a], d_recv.at[half, dp], d_sem.at[0], d_sem.at[1 + half],
                    device(z, core, oy, ox),
                )

            @pl.when(same)
            def _():
                d_recv[half, dp] = d_send[half, c, a]

    other = 1 - core
    loads[2].wait()
    feed(core, cls)
    wait(whole, c_sem.at[7])
    feed(other, cls)
    for step, (k, sem) in enumerate(((1, 4), (3, 3), (2, 5))):
        c = (cls + k) % 4
        arrived = normed.at[core, c]
        wait(arrived, c_sem.at[sem])
        send(arrived, arrived, c_sem.at[6], c_sem.at[8 + step], sibling)
        feed(core, c)
    for step, k in enumerate((1, 3, 2)):
        c = (cls + k) % 4
        wait(normed.at[other, c], c_sem.at[8 + step])
        feed(other, c)

    part = sq_part[...].reshape(32, 8, 128)
    folded = part + pltpu.roll(part, 64, 2)
    left = lax.broadcasted_iota(jnp.int32, (8, 128), 1) < 64
    sq_send[...] = jnp.where(left, folded[:16], folded[16:]).reshape(4, 4, 8, 128)
    for k in range(1, 16):
        oy, ox = (y + k // 4) % 4, (x + k % 4) % 4
        send(sq_send.at[(ox - oy + 4) % 4, oy], sq_recv.at[dp], sq_sem.at[0], sq_sem.at[1], plane(k))
    own_cls = (x - y + 4) % 4
    sq_recv[dp] = sq_send[own_cls, y]

    wait(sq_recv.at[0:15], sq_sem.at[1])
    squares = jnp.sum(sq_recv[...], axis=0)
    halves = []
    for half in range(2):
        wait(d_recv.at[0, 0:15], d_sem.at[1 + half])
        total = jnp.sum(d_recv[half].astype(F32), axis=0)
        mean = jnp.sum(jnp.where(left == (half == 0), squares, 0.0), axis=1, keepdims=True) / D
        scale = lax.rsqrt(mean + 1e-6)
        gate, up = total[:8] * scale, total[8:] * scale
        halves.append(gate / (1.0 + jnp.exp(-gate)) * up)
    hidden[own_cls, y] = jnp.concatenate(halves, axis=0).astype(BF16)
    mine = hidden.at[own_cls, y]
    for k in range(1, 16):
        send(mine, mine, h_sem.at[0], h_sem.at[1], plane(k))
    loads[3].wait()
    wait(d_recv.at[0, 0:15], h_sem.at[1])

    for k in (2, 1, 3, 0):
        c = (cls + k) % 4
        lowered = jnp.dot(hidden[c].reshape(64, 768), down[...], preferred_element_type=F32)
        lowered = lowered.reshape(4, 16, 512)
        first = core == 0
        g_own[c] = jnp.where(first, lowered[:, :8], lowered[:, 8:])
        sib_send[c] = to_tile(jnp.where(first, lowered[:, 8:], lowered[:, :8]))
        send(sib_send.at[c], sib_recv.at[c], sib_sem.at[0], sib_sem.at[1 + k], sibling)
    for k in (2, 1, 3, 0):
        c = (cls + k) % 4
        wait(sib_recv.at[c], sib_sem.at[1 + k])
        both = g_own[c] + from_tile(sib_recv[c])
        if k == 0:
            g1_own[...] = both
            continue
        g1_send[k - 1] = to_tile(both)
        if k == 2:
            for i, to in ((0, 2), (1, -2)):
                part = pl.ds(2 * i, 2)
                send(g1_send.at[1, part], g1_recv.at[1, part], g1_sem.at[0], g1_sem.at[2], ring(to))
        else:
            send(g1_send.at[k - 1], g1_recv.at[k - 1], g1_sem.at[0], g1_sem.at[k], ring(2 - k))
    total = g1_own[...]
    for k in (1, 3, 2):
        wait(g1_recv.at[k - 1], g1_sem.at[k])
        total = total + from_tile(g1_recv[k - 1])
    g1_own[...] = total
    g2_send[...] = to_tile(total)
    for k in (1, 2, 3):
        send(g2_send.at[(block + k) % 4], g2_recv.at[k - 1], g2_sem.at[0], g2_sem.at[1], ring(4 * k))
    wait(g2_recv, g2_sem.at[1])
    lowered = g1_own[block] + from_tile(jnp.sum(g2_recv[...].astype(F32), axis=0))
    out_ref[...] = (stream[...] + lowered).astype(BF16)

    wait(att.at[0:15], a_sem.at[0])
    wait(b_recv.at[0:7], b_sem.at[0])
    wait(normed.at[0, 0, 0:3], c_sem.at[0])
    wait(normed.at[0, 0:3], c_sem.at[2])
    wait(normed.at[0], c_sem.at[6])
    wait(d_recv.at[:, 0:15], d_sem.at[0])
    wait(sq_recv.at[0:15], sq_sem.at[0])
    wait(d_recv.at[0, 0:15], h_sem.at[0])
    wait(sib_recv, sib_sem.at[0])
    wait(g1_recv, g1_sem.at[0])
    wait(g2_recv, g2_sem.at[0])


def body(
    queries, fresh_kv, key_value_pages, page_table, lengths, cache_scales, residual, out_weight,
    norm_gain, gate_up, down_weight,
):
    vmem = pl.BlockSpec(memory_space=pltpu.VMEM)
    smem = pl.BlockSpec(memory_space=pltpu.SMEM)
    anywhere = pl.BlockSpec(memory_space=pl.ANY)
    sems = pltpu.SemaphoreType.DMA
    return pl.pallas_call(
        kernel,
        out_shape=jax.ShapeDtypeStruct((8, 512), BF16),
        in_specs=[vmem, vmem, anywhere, smem, smem, smem, vmem, anywhere, vmem, anywhere, anywhere],
        out_specs=vmem,
        scratch_shapes=[
            pltpu.VMEM((2, 24, 64, 128), BF16),
            pltpu.VMEM((1024, 512), BF16),
            pltpu.VMEM((2, 512, 768), BF16),
            pltpu.VMEM((768, 512), BF16),
            pltpu.VMEM((32, 128), F32),
            pltpu.VMEM((2, 8, 128), F32),
            pltpu.VMEM((16, 32, 128), BF16),
            pltpu.VMEM((8, 16, 256), BF16),
            pltpu.VMEM((8, 16, 256), BF16),
            pltpu.VMEM((8, 512), F32),
            pltpu.VMEM((2, 4, 4, 16, 256), BF16),
            pltpu.VMEM((2, 4, 4, 16, 768), BF16),
            pltpu.VMEM((2, 16, 16, 768), BF16),
            pltpu.VMEM((2, 4, 4, 8, 128), F32),
            pltpu.VMEM((4, 4, 8, 128), F32),
            pltpu.VMEM((16, 8, 128), F32),
            pltpu.VMEM((4, 4, 16, 768), BF16),
            pltpu.VMEM((4, 4, 8, 512), F32),
            pltpu.VMEM((4, 4, 16, 256), BF16),
            pltpu.VMEM((4, 4, 16, 256), BF16),
            pltpu.VMEM((3, 4, 16, 256), BF16),
            pltpu.VMEM((3, 4, 16, 256), BF16),
            pltpu.VMEM((4, 8, 512), F32),
            pltpu.VMEM((4, 16, 256), BF16),
            pltpu.VMEM((3, 16, 256), BF16),
            sems((4,)), sems((2,)), sems((2,)), sems((11,)), sems((3,)), sems((2,)), sems((2,)),
            sems((5,)), sems((4,)), sems((2,)),
        ],
        compiler_params=pltpu.CompilerParams(
            collective_id=0, has_side_effects=True, vmem_limit_bytes=40 << 20
        ),
        name="decode_layer",
    )(
        queries, fresh_kv, key_value_pages, page_table, lengths, cache_scales, residual,
        out_weight, norm_gain, gate_up, down_weight,
    )


def solution(mesh):
    placed = (
        P(("pool", "dp"), "head"),
        P(None, ("pool", "dp"), "head"),
        P(None, ("pool", "dp"), None, "head"),
        P(("pool", "dp"), None),
        P(("pool", "dp")),
        P(None, "head"),
        P(("pool", "head"), "dp"),
        P("head", "dp"),
        P("dp"),
        P(None, "dp", ("pool", "head")),
        P(("pool", "head"), "dp"),
    )
    return jax.shard_map(
        body, mesh=mesh, in_specs=placed, out_specs=P(("pool", "head"), "dp"), check_vma=False
    )
```

```python
import math

import jax
import jax.numpy as jnp
from jax import lax
from jax.experimental import pallas as pl
from jax.experimental.pallas import tpu as pltpu
from jax.sharding import PartitionSpec as P

D = 8192
HEAD_DIM = 128
MESH = pl.DeviceIdType.MESH
OFFSETS = (0, 1, -1, 2, -2, 3, -3, 4, -4, 5, -5, 6, -6, 7, -7, 8)
SLOT = {o % 16: i for i, o in enumerate(OFFSETS)}
GROUPS = ((0, 1), (1, 3), (3, 7), (7, 11), (11, 16))
ALONG_Z = (1, -1, 8, 7, -7, 6, -6, 5, -5, 4, -4, 3, -3, 2, -2)
NEAR = ((0, 1), (0, 3), (1, 0), (3, 0))
MIDDLE = ((0, 2), (2, 0), (1, 1), (1, 3), (3, 1), (3, 3))
FAR = ((1, 2), (2, 1), (3, 2), (2, 3), (2, 2))
F32 = jnp.float32
BF16 = jnp.bfloat16


def place():
    pool, dp, head = (lax.axis_index(name) for name in ("pool", "dp", "head"))
    return (pool // 2) * 8 + head, pool % 2, dp // 4, dp % 4


def device(z, core, y, x):
    return ((z // 8) * 2 + core, y * 4 + x, z % 8)


def send(src, dst, send_sem, recv_sem, to):
    pltpu.make_async_remote_copy(
        src_ref=src, dst_ref=dst, send_sem=send_sem, recv_sem=recv_sem,
        device_id=to, device_id_type=MESH,
    ).start()


def wait(ref, sem):
    pltpu.make_async_copy(ref, ref, sem).wait()


def to_tile(v):
    return jnp.concatenate([v[..., :256], v[..., 256:]], axis=-2).astype(BF16)


def from_tile(v):
    v = v.astype(F32)
    return jnp.concatenate([v[..., :8, :], v[..., 8:, :]], axis=-1)


def attend(q_ref, fresh_ref, kv, table, lengths, scales, q_rows, fresh_rows):
    q = q_ref[...].astype(F32)
    for g in range(8):
        q_rows[g * 4 : g * 4 + 4, :] = q[:, g * 128 : (g + 1) * 128]
    fresh = fresh_ref[...].astype(F32)
    for i in range(2):
        fresh_rows[i, 0:4, :] = fresh[i]
        fresh_rows[i, 4:8, :] = fresh[i]
    asked = q_rows[...]
    row = lax.broadcasted_iota(jnp.int32, (8, 1), 0) & 3
    column = lax.broadcasted_iota(jnp.int32, (8, 1536), 1)
    page, line = column >> 6, column & 63

    def by_request(values):
        a, b, c, d = values
        return jnp.where(row == 0, a, jnp.where(row == 1, b, jnp.where(row == 2, c, d)))

    length = by_request([lengths[t] for t in range(4)])
    live = jnp.zeros((8, 1536), jnp.bool_)
    for j in range(8):
        entry = by_request([table[t, j] for t in range(4)])
        live = live | ((page == entry) & (line < length - 64 * j))
    factor = 1.0 / math.sqrt(HEAD_DIM)
    keys = kv[0].reshape(1536, 128)
    scores = lax.dot_general(
        asked.astype(BF16), keys, (((1,), (1,)), ((), ())), preferred_element_type=F32
    ) * (scales[0, 0] * factor)
    scores = jnp.where(live[None], scores.reshape(4, 8, 1536), -jnp.inf)
    own = jnp.sum(asked.reshape(4, 8, 128) * fresh_rows[0][None], axis=2, keepdims=True) * factor
    top = jnp.maximum(jnp.max(scores, axis=2, keepdims=True), own)
    e = jnp.exp(scores - top)
    e_own = jnp.exp(own - top)
    total = jnp.sum(e, axis=2, keepdims=True) + e_own
    probs = (e / total).astype(BF16)
    own_prob = (e_own / total).astype(BF16).astype(F32)
    mixed = jnp.dot(
        probs.reshape(32, 1536), kv[1].reshape(1536, 128), preferred_element_type=F32
    ) * scales[0, 1]
    mixed = mixed.reshape(4, 8, 128) + own_prob * fresh_rows[1][None]
    return mixed.reshape(32, 128).astype(BF16)


def kernel(
    q_hbm, fresh_hbm, pages_hbm, table_hbm, lengths_hbm, scales_hbm, residual_hbm, out_w_hbm,
    gain_hbm, gate_up_hbm, down_hbm, out_ref,
    q_ref, fresh_ref, table, lengths, scales, residual_ref, gain_ref, kv, out_w, gate_up, down, q_rows, fresh_rows, att, b_send, b_recv, stream, normed,
    d_send, d_recv, sq_send, sq_recv, hidden, g_send, g_recv,
    load_sem, pair_sem, a_sem, b_sem, c_sem, d_sem, sq_sem, h_sem, g_sem,
):
    z, core, y, x = place()
    dp = y * 4 + x
    head = z % 8

    pairs = (
        (table_hbm, table), (lengths_hbm, lengths), (scales_hbm, scales), (q_hbm, q_ref),
        (fresh_hbm, fresh_ref), (pages_hbm, kv), (residual_hbm, residual_ref), (gain_hbm, gain_ref),
        (out_w_hbm, out_w), (gate_up_hbm, gate_up.at[core]), (down_hbm, down.at[core]),
    )
    loads = [
        pltpu.make_async_copy(src, dst, load_sem.at[i]) for i, (src, dst) in enumerate(pairs)
    ]
    for load in loads:
        load.start()

    def plane(dy, dx):
        return device(z, core, (y + dy) % 4, (x + dx) % 4)

    def ring(k):
        return device((z + k + 16) % 16, core, y, x)

    sibling = device(z, 1 - core, y, x)
    others = FAR[::-1] + MIDDLE + NEAR

    barrier = pltpu.get_barrier_semaphore()

    def greet(to):
        pl.semaphore_signal(barrier, inc=1, device_id=to, device_id_type=MESH)

    for k in range(1, 16):
        greet(ring(k))
    for step in others:
        greet(plane(*step))
    greet(sibling)

    for load in loads[:6]:
        load.wait()
    att[dp] = attend(q_ref, fresh_ref, kv, table, lengths, scales, q_rows, fresh_rows)
    pl.semaphore_wait(barrier, 31)
    for step in others:
        send(att.at[dp], att.at[dp], a_sem.at[0], a_sem.at[1], plane(*step))
    send(gate_up_hbm, gate_up.at[core], pair_sem.at[0], pair_sem.at[1], sibling)
    send(down_hbm, down.at[core], pair_sem.at[2], pair_sem.at[3], sibling)
    for load in loads[6:9]:
        load.wait()
    wait(att.at[0:15], a_sem.at[1])

    rows = att[...].astype(F32).reshape(8, 2, 4, 8, 128)
    even, odd = rows[:, 0], rows[:, 1]
    upper = lax.broadcasted_iota(jnp.int32, (8, 128), 0) < 4

    def swap(v):
        return pltpu.roll(v.reshape(32 * 8, 128).reshape(32, 8, 128), 4, 1).reshape(8, 4, 8, 128)

    low = jnp.where(upper, even, swap(odd))
    high = jnp.where(upper, swap(even), odd)
    columns = []
    for g in range(8):
        columns.append((low if g % 2 == 0 else high)[:, g // 2].reshape(64, 128))
    attended = jnp.concatenate(columns, axis=1).astype(BF16)
    projected = jnp.dot(attended, out_w[...], preferred_element_type=F32)
    b_send[...] = to_tile(projected.reshape(8, 8, 512))
    for i in range(7):
        up_to, down_to = 7 - i, i
        up_to = up_to - jnp.where(up_to <= head, 1, 0)
        down_to = down_to + jnp.where(down_to >= head, 1, 0)
        to = jnp.where(head < 4, up_to, down_to)
        send(b_send.at[to], b_recv.at[head], b_sem.at[0], b_sem.at[1], device((z // 8) * 8 + to, core, y, x))
    b_recv[head] = b_send[head]
    wait(b_recv.at[0:7], b_sem.at[1])
    summed = from_tile(jnp.sum(b_recv[...].astype(F32), axis=0))
    stream[...] = residual_ref[...].astype(F32) + summed

    gain = gain_ref[...].reshape(1, 512)
    normed[0] = to_tile(stream[...] * gain)
    for k in ALONG_Z:
        slot = SLOT[-k % 16]
        send(normed.at[0], normed.at[slot], c_sem.at[0], c_sem.at[slot], ring(k))

    inverse = 1.0 / (gain * gain)

    def feed(group):
        lo, hi = GROUPS[group]
        n = hi - lo
        for slot in range(max(lo, 1), hi):
            wait(normed.at[0], c_sem.at[slot])
        tokens = from_tile(normed[lo:hi]).reshape(8 * n, 512)
        squares = tokens * tokens * inverse
        squares = squares[:, :128] + squares[:, 128:256] + squares[:, 256:384] + squares[:, 384:]
        sq_send[lo:hi] = squares.reshape(n, 8, 128)
        lhs = tokens.astype(BF16)

        def both(i):
            parts = [jnp.dot(lhs, gate_up[c, i], preferred_element_type=F32) for c in range(2)]
            return jnp.concatenate(parts, axis=1).reshape(n, 8, 1536)

        d_send[lo:hi] = jnp.concatenate([both(0), both(1)], axis=1).astype(BF16)
        for slot in range(lo, hi):
            u = OFFSETS[slot] % 16
            oy, ox = u % 4, (u % 4 + u // 4) % 4
            same = dp == oy * 4 + ox

            @pl.when(jnp.logical_not(same))
            def _():
                to = device(z, core, oy, ox)
                send(d_send.at[slot], d_recv.at[dp], d_sem.at[0], d_sem.at[1], to)
                send(sq_send.at[slot], sq_recv.at[dp], sq_sem.at[0], sq_sem.at[1], to)

            @pl.when(same)
            def _():
                d_recv[dp] = d_send[slot]
                sq_recv[dp] = sq_send[slot]

    loads[9].wait()
    wait(gate_up.at[0], pair_sem.at[1])
    for group in range(5):
        feed(group)

    own = ((x - y + 4) % 4) * 4 + y
    wait(sq_recv.at[0:15], sq_sem.at[1])
    mean = jnp.sum(jnp.sum(sq_recv[...], axis=0), axis=1, keepdims=True) / D
    scale = lax.rsqrt(mean + 1e-6)
    wait(d_recv.at[0:15], d_sem.at[1])
    total = d_recv[0].astype(F32)
    for i in range(1, 16):
        total = total + d_recv[i].astype(F32)
    gate, up = total[:8] * scale, total[8:] * scale
    own_hidden = gate / (1.0 + jnp.exp(-gate)) * up
    hidden[own] = jnp.concatenate([own_hidden[:, :768], own_hidden[:, 768:]], axis=0).astype(BF16)
    mine = hidden.at[own]
    for steps, sem in ((FAR[::-1], 3), (MIDDLE, 2), (NEAR, 1)):
        for dy, dx in steps:
            send(mine, mine, h_sem.at[0], h_sem.at[sem], plane(-dy, -dx))
    loads[10].wait()
    wait(down.at[0], pair_sem.at[3])

    def lower(start, steps):
        n = len(steps)
        chips = [((x + dx - y - dy + 8) % 4) * 4 + (y + dy) % 4 for dy, dx in steps]
        tokens = jnp.concatenate([hidden[u][None] for u in chips], axis=0).astype(F32)
        lowered = jnp.zeros((8 * n, 512), F32)
        for c in range(2):
            lhs = tokens[:, 8 * c : 8 * c + 8].reshape(8 * n, 768).astype(BF16)
            lowered = lowered + jnp.dot(lhs, down[c], preferred_element_type=F32)
        g_send[pl.ds(start, n)] = to_tile(lowered.reshape(n, 8, 512))
        for i, u in enumerate(chips):

            @pl.when(u != 0)
            def _():
                send(g_send.at[start + i], g_recv.at[u], g_sem.at[0], g_sem.at[1], ring(u))

            @pl.when(u == 0)
            def _():
                g_recv[0] = g_send[start + i]

    wait(hidden.at[0:4], h_sem.at[1])
    lower(0, ((0, 0),) + NEAR)
    wait(hidden.at[0:6], h_sem.at[2])
    lower(5, MIDDLE)
    wait(hidden.at[0:5], h_sem.at[3])
    lower(11, FAR)
    wait(g_recv.at[1:16], g_sem.at[1])
    lowered = from_tile(jnp.sum(g_recv[...].astype(F32), axis=0))
    out_ref[...] = (stream[...] + lowered).astype(BF16)

    wait(gate_up.at[0], pair_sem.at[0])
    wait(down.at[0], pair_sem.at[2])
    wait(att.at[0:15], a_sem.at[0])
    wait(b_recv.at[0:7], b_sem.at[0])
    wait(normed.at[0:15], c_sem.at[0])
    wait(d_recv.at[0:15], d_sem.at[0])
    wait(sq_recv.at[0:15], sq_sem.at[0])
    wait(hidden.at[0:15], h_sem.at[0])
    wait(g_recv.at[0:15], g_sem.at[0])


def body(
    queries, fresh_kv, key_value_pages, page_table, lengths, cache_scales, residual, out_weight,
    norm_gain, gate_up, down_weight,
):
    vmem = pl.BlockSpec(memory_space=pltpu.VMEM)
    anywhere = pl.BlockSpec(memory_space=pl.ANY)
    sems = pltpu.SemaphoreType.DMA
    return pl.pallas_call(
        kernel,
        out_shape=jax.ShapeDtypeStruct((8, 512), BF16),
        in_specs=[anywhere] * 11,
        out_specs=vmem,
        scratch_shapes=[
            pltpu.VMEM((4, 1024), BF16),
            pltpu.VMEM((2, 4, 128), BF16),
            pltpu.SMEM((4, 8), jnp.int32),
            pltpu.SMEM((4,), jnp.int32),
            pltpu.SMEM((1, 2), F32),
            pltpu.VMEM((8, 512), BF16),
            pltpu.VMEM((512,), F32),
            pltpu.VMEM((2, 24, 64, 128), BF16),
            pltpu.VMEM((1024, 512), BF16),
            pltpu.VMEM((2, 2, 512, 768), BF16),
            pltpu.VMEM((2, 768, 512), BF16),
            pltpu.VMEM((32, 128), F32),
            pltpu.VMEM((2, 8, 128), F32),
            pltpu.VMEM((16, 32, 128), BF16),
            pltpu.VMEM((8, 16, 256), BF16),
            pltpu.VMEM((8, 16, 256), BF16),
            pltpu.VMEM((8, 512), F32),
            pltpu.VMEM((16, 16, 256), BF16),
            pltpu.VMEM((16, 16, 1536), BF16),
            pltpu.VMEM((16, 16, 1536), BF16),
            pltpu.VMEM((16, 8, 128), F32),
            pltpu.VMEM((16, 8, 128), F32),
            pltpu.VMEM((16, 16, 768), BF16),
            pltpu.VMEM((16, 16, 256), BF16),
            pltpu.VMEM((16, 16, 256), BF16),
            sems((11,)), sems((4,)), sems((2,)), sems((2,)), sems((16,)), sems((2,)), sems((2,)),
            sems((4,)), sems((2,)),
        ],
        compiler_params=pltpu.CompilerParams(
            collective_id=0, has_side_effects=True, vmem_limit_bytes=64 << 20
        ),
        name="decode_layer",
    )(
        queries, fresh_kv, key_value_pages, page_table, lengths, cache_scales.T, residual,
        out_weight, norm_gain, gate_up, down_weight,
    )


def solution(mesh):
    placed = (
        P(("pool", "dp"), "head"),
        P(None, ("pool", "dp"), "head"),
        P(None, ("pool", "dp"), None, "head"),
        P(("pool", "dp"), None),
        P(("pool", "dp")),
        P(None, "head"),
        P(("pool", "head"), "dp"),
        P("head", "dp"),
        P("dp"),
        P(None, "dp", ("pool", "head")),
        P(("pool", "head"), "dp"),
    )
    return jax.shard_map(
        body, mesh=mesh, in_specs=placed, out_specs=P(("pool", "head"), "dp"), check_vma=False
    )
```

```python
import math

import jax
import jax.numpy as jnp
from jax import lax
from jax.experimental import pallas as pl
from jax.experimental.pallas import tpu as pltpu
from jax.sharding import PartitionSpec as P

D = 8192
HEAD_DIM = 128
MESH = pl.DeviceIdType.MESH
OFFSETS = (0, 1, -1, 2, -2, 3, -3, 4, -4, 5, -5, 6, -6, 7, -7, 8)
SLOT = {o % 16: i for i, o in enumerate(OFFSETS)}
GROUPS = ((0, 1), (1, 3), (3, 8), (8, 12), (12, 16))
ALONG_Z = (1, -1, 8, 7, -7, 6, -6, 5, -5, 4, -4, 3, -3, 2, -2)
NEAR = ((0, 1), (0, 3), (1, 0), (3, 0))
MIDDLE = ((0, 2), (2, 0), (1, 1), (1, 3), (3, 1), (3, 3))
FAR = ((1, 2), (2, 1), (3, 2), (2, 3), (2, 2))
F32 = jnp.float32
BF16 = jnp.bfloat16


def place():
    pool, dp, head = (lax.axis_index(name) for name in ("pool", "dp", "head"))
    return (pool // 2) * 8 + head, pool % 2, dp // 4, dp % 4


def device(z, core, y, x):
    return ((z // 8) * 2 + core, y * 4 + x, z % 8)


def send(src, dst, send_sem, recv_sem, to):
    pltpu.make_async_remote_copy(
        src_ref=src, dst_ref=dst, send_sem=send_sem, recv_sem=recv_sem,
        device_id=to, device_id_type=MESH,
    ).start()


def wait(ref, sem):
    pltpu.make_async_copy(ref, ref, sem).wait()


def to_tile(v):
    return jnp.concatenate([v[..., :256], v[..., 256:]], axis=-2).astype(BF16)


def from_tile(v):
    v = v.astype(F32)
    return jnp.concatenate([v[..., :8, :], v[..., 8:, :]], axis=-1)


def attend(q_ref, fresh_ref, kv, table, lengths, scales, q_rows, fresh_rows):
    q = q_ref[...].astype(F32)
    for g in range(8):
        q_rows[g * 4 : g * 4 + 4, :] = q[:, g * 128 : (g + 1) * 128]
    fresh = fresh_ref[...].astype(F32)
    for i in range(2):
        fresh_rows[i, 0:4, :] = fresh[i]
        fresh_rows[i, 4:8, :] = fresh[i]
    asked = q_rows[...]
    row = lax.broadcasted_iota(jnp.int32, (8, 1), 0) & 3
    column = lax.broadcasted_iota(jnp.int32, (8, 1536), 1)
    page, line = column >> 6, column & 63

    def by_request(values):
        a, b, c, d = values
        return jnp.where(row == 0, a, jnp.where(row == 1, b, jnp.where(row == 2, c, d)))

    length = by_request([lengths[t] for t in range(4)])
    live = jnp.zeros((8, 1536), jnp.bool_)
    for j in range(8):
        entry = by_request([table[t, j] for t in range(4)])
        live = live | ((page == entry) & (line < length - 64 * j))
    factor = 1.0 / math.sqrt(HEAD_DIM)
    keys = kv[0].reshape(1536, 128)
    scores = lax.dot_general(
        asked.astype(BF16), keys, (((1,), (1,)), ((), ())), preferred_element_type=F32
    ) * (scales[0, 0] * factor)
    scores = jnp.where(live[None], scores.reshape(4, 8, 1536), -jnp.inf)
    own = jnp.sum(asked.reshape(4, 8, 128) * fresh_rows[0][None], axis=2, keepdims=True) * factor
    top = jnp.maximum(jnp.max(scores, axis=2, keepdims=True), own)
    e = jnp.exp(scores - top)
    e_own = jnp.exp(own - top)
    total = jnp.sum(e, axis=2, keepdims=True) + e_own
    probs = (e / total).astype(BF16)
    own_prob = (e_own / total).astype(BF16).astype(F32)
    mixed = jnp.dot(
        probs.reshape(32, 1536), kv[1].reshape(1536, 128), preferred_element_type=F32
    ) * scales[0, 1]
    mixed = mixed.reshape(4, 8, 128) + own_prob * fresh_rows[1][None]
    return mixed.reshape(32, 128).astype(BF16)


def kernel(
    q_hbm, fresh_hbm, pages_hbm, table_hbm, lengths_hbm, scales_hbm, residual_hbm, out_w_hbm,
    gain_hbm, gate_up_hbm, down_hbm, out_ref,
    q_ref, fresh_ref, table, lengths, scales, residual_ref, gain_ref, kv, out_w, gate_up, down, q_rows, fresh_rows, att, b_send, b_recv, stream, normed,
    d_send, d_recv, sq_send, sq_recv, scale_send, scale_recv, hidden,
    g_send, g_recv,
    load_sem, pair_sem, a_sem, b_sem, c_sem, d_sem, sq_sem, scale_sem,
    h_sem, g_sem,
):
    z, core, y, x = place()
    dp = y * 4 + x
    head = z % 8

    pairs = (
        (table_hbm, table), (lengths_hbm, lengths), (scales_hbm, scales), (q_hbm, q_ref),
        (fresh_hbm, fresh_ref), (pages_hbm, kv), (residual_hbm, residual_ref), (gain_hbm, gain_ref),
        (out_w_hbm, out_w), (gate_up_hbm, gate_up.at[core]), (down_hbm, down.at[core]),
    )
    loads = [
        pltpu.make_async_copy(src, dst, load_sem.at[i]) for i, (src, dst) in enumerate(pairs)
    ]
    for load in loads:
        load.start()

    def plane(dy, dx):
        return device(z, core, (y + dy) % 4, (x + dx) % 4)

    def ring(k):
        return device((z + k + 16) % 16, core, y, x)

    sibling = device(z, 1 - core, y, x)
    others = FAR[::-1] + MIDDLE + NEAR

    barrier = pltpu.get_barrier_semaphore()

    def greet(to):
        pl.semaphore_signal(barrier, inc=1, device_id=to, device_id_type=MESH)

    for k in range(1, 16):
        greet(ring(k))
    for step in others:
        greet(plane(*step))
    greet(sibling)

    for load in loads[:6]:
        load.wait()
    att[dp] = attend(q_ref, fresh_ref, kv, table, lengths, scales, q_rows, fresh_rows)
    pl.semaphore_wait(barrier, 31)
    for step in others:
        send(att.at[dp], att.at[dp], a_sem.at[0], a_sem.at[1], plane(*step))
    send(gate_up_hbm, gate_up.at[core], pair_sem.at[0], pair_sem.at[1], sibling)
    send(down_hbm, down.at[core], pair_sem.at[2], pair_sem.at[3], sibling)
    for load in loads[6:9]:
        load.wait()
    wait(att.at[0:15], a_sem.at[1])

    rows = att[...].astype(F32).reshape(8, 2, 4, 8, 128)
    even, odd = rows[:, 0], rows[:, 1]
    upper = lax.broadcasted_iota(jnp.int32, (8, 128), 0) < 4

    def swap(v):
        return pltpu.roll(v.reshape(32 * 8, 128).reshape(32, 8, 128), 4, 1).reshape(8, 4, 8, 128)

    low = jnp.where(upper, even, swap(odd))
    high = jnp.where(upper, swap(even), odd)
    columns = []
    for g in range(8):
        columns.append((low if g % 2 == 0 else high)[:, g // 2].reshape(64, 128))
    attended = jnp.concatenate(columns, axis=1).astype(BF16)
    projected = jnp.dot(attended, out_w[...], preferred_element_type=F32)
    b_send[...] = to_tile(projected.reshape(8, 8, 512))
    for i in range(7):
        up_to, down_to = 7 - i, i
        up_to = up_to - jnp.where(up_to <= head, 1, 0)
        down_to = down_to + jnp.where(down_to >= head, 1, 0)
        to = jnp.where(head < 4, up_to, down_to)
        send(b_send.at[to], b_recv.at[head], b_sem.at[0], b_sem.at[1], device((z // 8) * 8 + to, core, y, x))
    b_recv[head] = b_send[head]
    wait(b_recv.at[0:7], b_sem.at[1])
    summed = from_tile(jnp.sum(b_recv[...].astype(F32), axis=0))
    stream[...] = residual_ref[...].astype(F32) + summed

    gain = gain_ref[...].reshape(1, 512)
    normed[0] = to_tile(stream[...] * gain)
    for k in ALONG_Z:
        slot = SLOT[-k % 16]
        send(normed.at[0], normed.at[slot], c_sem.at[0], c_sem.at[slot], ring(k))

    squares = stream[...] * stream[...]
    sq_send[...] = squares[:, :128] + squares[:, 128:256] + squares[:, 256:384] + squares[:, 384:]
    for step in others:
        send(sq_send, sq_recv.at[dp], sq_sem.at[0], sq_sem.at[1], plane(*step))
    sq_recv[dp] = sq_send[...]

    unit = ((x - y + 4) % 4) * 4 + y
    unit_chip, unit_core = unit // 2, unit % 2

    def unit_ring(phase):
        slot = 8 * phase + unit_chip
        return ((slot + 1) // 2) * (2 * (slot % 2) - 1)

    def scales_out():
        wait(sq_recv.at[0:15], sq_sem.at[1])
        mean = jnp.sum(jnp.sum(sq_recv[...], axis=0), axis=1, keepdims=True) / D
        scale_send[...] = jnp.broadcast_to(lax.rsqrt(mean + 1e-6), (8, 128))
        send(scale_send, scale_recv.at[1], scale_sem.at[0], scale_sem.at[2], ring(-unit_ring(1)))

        @pl.when(unit_chip != 0)
        def _():
            send(scale_send, scale_recv.at[0], scale_sem.at[0], scale_sem.at[1], ring(-unit_ring(0)))

        @pl.when(unit_chip == 0)
        def _():
            scale_recv[0] = scale_send[...]

    def feed(group):
        lo, hi = GROUPS[group]
        n = hi - lo
        for slot in range(max(lo, 1), hi):
            wait(normed.at[0], c_sem.at[slot])
        lhs = from_tile(normed[lo:hi]).reshape(8 * n, 512).astype(BF16)
        for c in range(2):
            gate = jnp.dot(lhs, gate_up[c, 0], preferred_element_type=F32).reshape(n, 8, 768)
            up = jnp.dot(lhs, gate_up[c, 1], preferred_element_type=F32).reshape(n, 8, 768)
            d_send[c, lo:hi] = jnp.concatenate([gate, up], axis=1).astype(BF16)
        for slot in range(lo, hi):
            phase = slot // 8
            for c in range(2):
                u = 2 * (slot % 8) + c
                oy, ox = u % 4, (u % 4 + u // 4) % 4
                same = dp == oy * 4 + ox

                @pl.when(jnp.logical_not(same))
                def _():
                    send(
                        d_send.at[c, slot], d_recv.at[phase, dp], d_sem.at[0], d_sem.at[1 + phase],
                        device(z, core, oy, ox),
                    )

                @pl.when(same)
                def _():
                    d_recv[phase, dp] = d_send[c, slot]

    def share_hidden(phase):
        if phase == 0:

            @pl.when(unit_chip != 0)
            def _():
                wait(scale_send, scale_sem.at[1])
        else:
            wait(scale_send, scale_sem.at[2])
        scale = scale_recv[phase][:, :1]
        wait(d_recv.at[0, 0:15], d_sem.at[1 + phase])
        total = d_recv[phase, 0].astype(F32)
        for i in range(1, 16):
            total = total + d_recv[phase, i].astype(F32)
        gate, up = total[:8] * scale, total[8:] * scale
        own = gate / (1.0 + jnp.exp(-gate)) * up
        hidden[phase, unit_core, unit_chip] = jnp.concatenate([own[:, :384], own[:, 384:]], axis=0).astype(BF16)
        mine = hidden.at[phase, unit_core, unit_chip]
        for step in others:
            send(mine, mine, h_sem.at[0], h_sem.at[1 + phase], plane(*step))

    def lower(phase):
        wait(d_recv.at[0, 0:15, :, 0:384], h_sem.at[1 + phase])
        lowered = jnp.zeros((64, 512), F32)
        for c in range(2):
            tokens = hidden[phase, c].astype(F32)
            lhs = jnp.concatenate([tokens[:, :8], tokens[:, 8:]], axis=2).reshape(64, 768).astype(BF16)
            lowered = lowered + jnp.dot(lhs, down[c], preferred_element_type=F32)
        g_send[8 * phase : 8 * phase + 8] = to_tile(lowered.reshape(8, 8, 512))
        for slot in range(8 * phase + 7, 8 * phase - 1, -1):
            if slot == 0:
                g_recv[0] = g_send[0]
            else:
                send(g_send.at[slot], g_recv.at[slot], g_sem.at[0], g_sem.at[1], ring(OFFSETS[slot]))

    loads[9].wait()
    wait(gate_up.at[0], pair_sem.at[1])
    feed(0)
    feed(1)
    scales_out()
    feed(2)
    feed(3)
    feed(4)
    share_hidden(0)
    share_hidden(1)
    loads[10].wait()
    wait(down.at[0], pair_sem.at[3])
    lower(0)
    lower(1)
    wait(g_recv.at[1:16], g_sem.at[1])
    lowered = from_tile(jnp.sum(g_recv[...].astype(F32), axis=0))
    out_ref[...] = (stream[...] + lowered).astype(BF16)

    wait(gate_up.at[0], pair_sem.at[0])
    wait(down.at[0], pair_sem.at[2])
    wait(att.at[0:15], a_sem.at[0])
    wait(b_recv.at[0:7], b_sem.at[0])
    wait(normed.at[0:15], c_sem.at[0])
    wait(d_recv.at[:, 0:15], d_sem.at[0])
    wait(sq_recv.at[0:15], sq_sem.at[0])
    wait(scale_send, scale_sem.at[0])

    @pl.when(unit_chip != 0)
    def _():
        wait(scale_send, scale_sem.at[0])

    wait(d_recv.at[0, 0:15], h_sem.at[0])
    wait(g_recv.at[0:15], g_sem.at[0])


def body(
    queries, fresh_kv, key_value_pages, page_table, lengths, cache_scales, residual, out_weight,
    norm_gain, gate_up, down_weight,
):
    vmem = pl.BlockSpec(memory_space=pltpu.VMEM)
    anywhere = pl.BlockSpec(memory_space=pl.ANY)
    sems = pltpu.SemaphoreType.DMA
    return pl.pallas_call(
        kernel,
        out_shape=jax.ShapeDtypeStruct((8, 512), BF16),
        in_specs=[anywhere] * 11,
        out_specs=vmem,
        scratch_shapes=[
            pltpu.VMEM((4, 1024), BF16),
            pltpu.VMEM((2, 4, 128), BF16),
            pltpu.SMEM((4, 8), jnp.int32),
            pltpu.SMEM((4,), jnp.int32),
            pltpu.SMEM((1, 2), F32),
            pltpu.VMEM((8, 512), BF16),
            pltpu.VMEM((512,), F32),
            pltpu.VMEM((2, 24, 64, 128), BF16),
            pltpu.VMEM((1024, 512), BF16),
            pltpu.VMEM((2, 2, 512, 768), BF16),
            pltpu.VMEM((2, 768, 512), BF16),
            pltpu.VMEM((32, 128), F32),
            pltpu.VMEM((2, 8, 128), F32),
            pltpu.VMEM((16, 32, 128), BF16),
            pltpu.VMEM((8, 16, 256), BF16),
            pltpu.VMEM((8, 16, 256), BF16),
            pltpu.VMEM((8, 512), F32),
            pltpu.VMEM((16, 16, 256), BF16),
            pltpu.VMEM((2, 16, 16, 768), BF16),
            pltpu.VMEM((2, 16, 16, 768), BF16),
            pltpu.VMEM((8, 128), F32),
            pltpu.VMEM((16, 8, 128), F32),
            pltpu.VMEM((8, 128), F32),
            pltpu.VMEM((2, 8, 128), F32),
            pltpu.VMEM((2, 2, 8, 16, 384), BF16),
            pltpu.VMEM((16, 16, 256), BF16),
            pltpu.VMEM((16, 16, 256), BF16),
            sems((11,)), sems((4,)), sems((2,)), sems((2,)), sems((16,)), sems((3,)), sems((2,)),
            sems((3,)), sems((3,)), sems((2,)),
        ],
        compiler_params=pltpu.CompilerParams(
            collective_id=0, has_side_effects=True, vmem_limit_bytes=64 << 20
        ),
        name="decode_layer",
    )(
        queries, fresh_kv, key_value_pages, page_table, lengths, cache_scales.T, residual,
        out_weight, norm_gain, gate_up, down_weight,
    )


def solution(mesh):
    placed = (
        P(("pool", "dp"), "head"),
        P(None, ("pool", "dp"), "head"),
        P(None, ("pool", "dp"), None, "head"),
        P(("pool", "dp"), None),
        P(("pool", "dp")),
        P(None, "head"),
        P(("pool", "head"), "dp"),
        P("head", "dp"),
        P("dp"),
        P(None, "dp", ("pool", "head")),
        P(("pool", "head"), "dp"),
    )
    return jax.shard_map(
        body, mesh=mesh, in_specs=placed, out_specs=P(("pool", "head"), "dp"), check_vma=False
    )
```

```python
import math

import jax
import jax.numpy as jnp
from jax import lax
from jax.experimental import pallas as pl
from jax.experimental.pallas import tpu as pltpu
from jax.sharding import PartitionSpec as P

D = 8192
HEAD_DIM = 128
MESH = pl.DeviceIdType.MESH
OFFSETS = (0, 1, -1, 2, -2, 3, -3, 4, -4, 5, -5, 6, -6, 7, -7, 8)
SLOT = {o % 16: i for i, o in enumerate(OFFSETS)}
GROUPS = ((0, 3), (3, 8), (8, 16))
ALONG_Z = (1, -1, 8, 7, -7, 6, -6, 5, -5, 4, -4, 3, -3, 2, -2)
NEAR = ((0, 1), (0, 3), (1, 0), (3, 0))
MIDDLE = ((0, 2), (2, 0), (1, 1), (1, 3), (3, 1), (3, 3))
FAR = ((1, 2), (2, 1), (3, 2), (2, 3), (2, 2))
F32 = jnp.float32
BF16 = jnp.bfloat16


def place():
    pool, dp, head = (lax.axis_index(name) for name in ("pool", "dp", "head"))
    return (pool // 2) * 8 + head, pool % 2, dp // 4, dp % 4


def device(z, core, y, x):
    return ((z // 8) * 2 + core, y * 4 + x, z % 8)


def send(src, dst, send_sem, recv_sem, to):
    pltpu.make_async_remote_copy(
        src_ref=src, dst_ref=dst, send_sem=send_sem, recv_sem=recv_sem,
        device_id=to, device_id_type=MESH,
    ).start()


def wait(ref, sem):
    pltpu.make_async_copy(ref, ref, sem).wait()


def to_tile(v):
    return jnp.concatenate([v[..., :256], v[..., 256:]], axis=-2).astype(BF16)


def from_tile(v):
    v = v.astype(F32)
    return jnp.concatenate([v[..., :8, :], v[..., 8:, :]], axis=-1)


def attend(q_ref, fresh_ref, kv, table, lengths, scales, q_rows, fresh_rows):
    q = q_ref[...].astype(F32)
    for g in range(8):
        q_rows[g * 4 : g * 4 + 4, :] = q[:, g * 128 : (g + 1) * 128]
    fresh = fresh_ref[...].astype(F32)
    for i in range(2):
        fresh_rows[i, 0:4, :] = fresh[i]
        fresh_rows[i, 4:8, :] = fresh[i]
    asked = q_rows[...]
    row = lax.broadcasted_iota(jnp.int32, (8, 1), 0) & 3
    column = lax.broadcasted_iota(jnp.int32, (8, 1536), 1)
    page, line = column >> 6, column & 63

    def by_request(values):
        a, b, c, d = values
        return jnp.where(row == 0, a, jnp.where(row == 1, b, jnp.where(row == 2, c, d)))

    length = by_request([lengths[t] for t in range(4)])
    live = jnp.zeros((8, 1536), jnp.bool_)
    for j in range(8):
        entry = by_request([table[t, j] for t in range(4)])
        live = live | ((page == entry) & (line < length - 64 * j))
    factor = 1.0 / math.sqrt(HEAD_DIM)
    keys = kv[0].reshape(1536, 128)
    scores = lax.dot_general(
        asked.astype(BF16), keys, (((1,), (1,)), ((), ())), preferred_element_type=F32
    ) * (scales[0, 0] * factor)
    scores = jnp.where(live[None], scores.reshape(4, 8, 1536), -jnp.inf)
    own = jnp.sum(asked.reshape(4, 8, 128) * fresh_rows[0][None], axis=2, keepdims=True) * factor
    top = jnp.maximum(jnp.max(scores, axis=2, keepdims=True), own)
    e = jnp.exp(scores - top)
    e_own = jnp.exp(own - top)
    total = jnp.sum(e, axis=2, keepdims=True) + e_own
    probs = (e / total).astype(BF16)
    own_prob = (e_own / total).astype(BF16).astype(F32)
    mixed = jnp.dot(
        probs.reshape(32, 1536), kv[1].reshape(1536, 128), preferred_element_type=F32
    ) * scales[0, 1]
    mixed = mixed.reshape(4, 8, 128) + own_prob * fresh_rows[1][None]
    return mixed.reshape(32, 128).astype(BF16)


def kernel(
    q_hbm, fresh_hbm, pages_hbm, table_hbm, lengths_hbm, scales_hbm, residual_hbm, out_w_hbm,
    gain_hbm, gate_up_hbm, down_hbm, out_ref,
    q_ref, fresh_ref, table, lengths, scales, residual_ref, gain_ref, kv, out_w, gate_up, down, q_rows, fresh_rows, att, b_send, b_recv, stream, normed,
    d_send, d_recv, sq_send, sq_recv, scale_send, scale_recv, hidden,
    g_send, g_recv,
    load_sem, pair_sem, a_sem, b_sem, c_sem, d_sem, sq_sem, scale_sem,
    h_sem, g_sem,
):
    z, core, y, x = place()
    dp = y * 4 + x
    head = z % 8

    pairs = (
        (table_hbm, table), (lengths_hbm, lengths), (scales_hbm, scales), (q_hbm, q_ref),
        (fresh_hbm, fresh_ref), (pages_hbm, kv), (residual_hbm, residual_ref), (gain_hbm, gain_ref),
        (out_w_hbm, out_w), (gate_up_hbm, gate_up.at[core]), (down_hbm, down.at[core]),
    )
    loads = [
        pltpu.make_async_copy(src, dst, load_sem.at[i]) for i, (src, dst) in enumerate(pairs)
    ]
    for load in loads:
        load.start()

    def plane(dy, dx):
        return device(z, core, (y + dy) % 4, (x + dx) % 4)

    def ring(k):
        return device((z + k + 16) % 16, core, y, x)

    sibling = device(z, 1 - core, y, x)
    others = FAR[::-1] + MIDDLE + NEAR

    barrier = pltpu.get_barrier_semaphore()

    def greet(to):
        pl.semaphore_signal(barrier, inc=1, device_id=to, device_id_type=MESH)

    for k in sorted(ALONG_Z, key=abs, reverse=True):
        greet(ring(k))
    for step in others:
        greet(plane(*step))
    greet(sibling)

    for load in loads[:6]:
        load.wait()
    att[dp] = attend(q_ref, fresh_ref, kv, table, lengths, scales, q_rows, fresh_rows)
    pl.semaphore_wait(barrier, 31)
    for step in others:
        send(att.at[dp], att.at[dp], a_sem.at[0], a_sem.at[1], plane(*step))
    send(gate_up_hbm, gate_up.at[core], pair_sem.at[0], pair_sem.at[1], sibling)
    for load in loads[6:9]:
        load.wait()
    wait(att.at[0:15], a_sem.at[1])

    rows = att[...].astype(F32).reshape(8, 2, 4, 8, 128)
    even, odd = rows[:, 0], rows[:, 1]
    upper = lax.broadcasted_iota(jnp.int32, (8, 128), 0) < 4

    def swap(v):
        return pltpu.roll(v.reshape(32 * 8, 128).reshape(32, 8, 128), 4, 1).reshape(8, 4, 8, 128)

    low = jnp.where(upper, even, swap(odd))
    high = jnp.where(upper, swap(even), odd)
    columns = []
    for g in range(8):
        columns.append((low if g % 2 == 0 else high)[:, g // 2].reshape(64, 128))
    attended = jnp.concatenate(columns, axis=1).astype(BF16)
    projected = jnp.dot(attended, out_w[...], preferred_element_type=F32)
    b_send[...] = to_tile(projected.reshape(8, 8, 512))
    for i in range(7):
        up_to, down_to = 7 - i, i
        up_to = up_to - jnp.where(up_to <= head, 1, 0)
        down_to = down_to + jnp.where(down_to >= head, 1, 0)
        to = jnp.where(head < 4, up_to, down_to)
        send(b_send.at[to], b_recv.at[head], b_sem.at[0], b_sem.at[1], device((z // 8) * 8 + to, core, y, x))
    b_recv[head] = b_send[head]
    send(down_hbm, down.at[core], pair_sem.at[2], pair_sem.at[3], sibling)
    wait(b_recv.at[0:7], b_sem.at[1])
    summed = from_tile(jnp.sum(b_recv[...].astype(F32), axis=0))
    stream[...] = residual_ref[...].astype(F32) + summed

    gain = gain_ref[...].reshape(1, 512)
    normed[0] = to_tile(stream[...] * gain)
    for k in ALONG_Z:
        slot = SLOT[-k % 16]
        send(normed.at[0], normed.at[slot], c_sem.at[0], c_sem.at[slot], ring(k))

    squares = stream[...] * stream[...]
    sq_send[...] = squares[:, :128] + squares[:, 128:256] + squares[:, 256:384] + squares[:, 384:]
    for step in others:
        send(sq_send, sq_recv.at[dp], sq_sem.at[0], sq_sem.at[1], plane(*step))
    sq_recv[dp] = sq_send[...]

    unit = ((x - y + 4) % 4) * 4 + y
    unit_chip, unit_core = unit // 2, unit % 2

    def unit_ring(phase):
        slot = 8 * phase + unit_chip
        return ((slot + 1) // 2) * (2 * (slot % 2) - 1)

    def scales_out():
        wait(sq_recv.at[0:15], sq_sem.at[1])
        mean = jnp.sum(jnp.sum(sq_recv[...], axis=0), axis=1, keepdims=True) / D
        scale_send[...] = jnp.broadcast_to(lax.rsqrt(mean + 1e-6), (8, 128))
        send(scale_send, scale_recv.at[1], scale_sem.at[0], scale_sem.at[2], ring(-unit_ring(1)))

        @pl.when(unit_chip != 0)
        def _():
            send(scale_send, scale_recv.at[0], scale_sem.at[0], scale_sem.at[1], ring(-unit_ring(0)))

        @pl.when(unit_chip == 0)
        def _():
            scale_recv[0] = scale_send[...]

    def feed(group):
        lo, hi = GROUPS[group]
        n = hi - lo
        for slot in range(max(lo, 1), hi):
            wait(normed.at[0], c_sem.at[slot])
        lhs = from_tile(normed[lo:hi]).reshape(8 * n, 512).astype(BF16)
        for c in range(2):
            gate = jnp.dot(lhs, gate_up[c, 0], preferred_element_type=F32).reshape(n, 8, 768)
            up = jnp.dot(lhs, gate_up[c, 1], preferred_element_type=F32).reshape(n, 8, 768)
            d_send[c, lo:hi] = jnp.concatenate([gate, up], axis=1).astype(BF16)
        for slot in range(lo, hi):
            phase = slot // 8
            for c in range(2):
                u = 2 * (slot % 8) + c
                oy, ox = u % 4, (u % 4 + u // 4) % 4
                same = dp == oy * 4 + ox

                @pl.when(jnp.logical_not(same))
                def _():
                    send(
                        d_send.at[c, slot], d_recv.at[phase, dp], d_sem.at[0], d_sem.at[1 + phase],
                        device(z, core, oy, ox),
                    )

                @pl.when(same)
                def _():
                    d_recv[phase, dp] = d_send[c, slot]

    def share_hidden(phase):
        if phase == 0:

            @pl.when(unit_chip != 0)
            def _():
                wait(scale_send, scale_sem.at[1])
        else:
            wait(scale_send, scale_sem.at[2])
        scale = scale_recv[phase][:, :1]
        wait(d_recv.at[0, 0:15], d_sem.at[1 + phase])
        total = d_recv[phase, 0].astype(F32)
        for i in range(1, 16):
            total = total + d_recv[phase, i].astype(F32)
        gate, up = total[:8] * scale, total[8:] * scale
        own = gate / (1.0 + jnp.exp(-gate)) * up
        hidden[phase, unit_core, unit_chip] = jnp.concatenate([own[:, :384], own[:, 384:]], axis=0).astype(BF16)
        mine = hidden.at[phase, unit_core, unit_chip]
        for step in others:
            send(mine, mine, h_sem.at[0], h_sem.at[1 + phase], plane(*step))

    def lower(phase):
        wait(d_recv.at[0, 0:15, :, 0:384], h_sem.at[1 + phase])
        lowered = jnp.zeros((64, 512), F32)
        for c in range(2):
            tokens = hidden[phase, c].astype(F32)
            lhs = jnp.concatenate([tokens[:, :8], tokens[:, 8:]], axis=2).reshape(64, 768).astype(BF16)
            lowered = lowered + jnp.dot(lhs, down[c], preferred_element_type=F32)
        g_send[8 * phase : 8 * phase + 8] = to_tile(lowered.reshape(8, 8, 512))
        for slot in range(8 * phase + 7, 8 * phase - 1, -1):
            if slot == 0:
                g_recv[0] = g_send[0]
            else:
                send(g_send.at[slot], g_recv.at[slot], g_sem.at[0], g_sem.at[1], ring(OFFSETS[slot]))

    loads[9].wait()
    wait(gate_up.at[0], pair_sem.at[1])
    feed(0)
    feed(1)
    scales_out()
    feed(2)
    share_hidden(0)
    share_hidden(1)
    loads[10].wait()
    wait(down.at[0], pair_sem.at[3])
    lower(0)
    lower(1)
    wait(g_recv.at[1:16], g_sem.at[1])
    lowered = from_tile(jnp.sum(g_recv[...].astype(F32), axis=0))
    out_ref[...] = (stream[...] + lowered).astype(BF16)

    wait(gate_up.at[0], pair_sem.at[0])
    wait(down.at[0], pair_sem.at[2])
    wait(att.at[0:15], a_sem.at[0])
    wait(b_recv.at[0:7], b_sem.at[0])
    wait(normed.at[0:15], c_sem.at[0])
    wait(d_recv.at[:, 0:15], d_sem.at[0])
    wait(sq_recv.at[0:15], sq_sem.at[0])
    wait(scale_send, scale_sem.at[0])

    @pl.when(unit_chip != 0)
    def _():
        wait(scale_send, scale_sem.at[0])

    wait(d_recv.at[0, 0:15], h_sem.at[0])
    wait(g_recv.at[0:15], g_sem.at[0])


def body(
    queries, fresh_kv, key_value_pages, page_table, lengths, cache_scales, residual, out_weight,
    norm_gain, gate_up, down_weight,
):
    vmem = pl.BlockSpec(memory_space=pltpu.VMEM)
    anywhere = pl.BlockSpec(memory_space=pl.ANY)
    sems = pltpu.SemaphoreType.DMA
    return pl.pallas_call(
        kernel,
        out_shape=jax.ShapeDtypeStruct((8, 512), BF16),
        in_specs=[anywhere] * 11,
        out_specs=vmem,
        scratch_shapes=[
            pltpu.VMEM((4, 1024), BF16),
            pltpu.VMEM((2, 4, 128), BF16),
            pltpu.SMEM((4, 8), jnp.int32),
            pltpu.SMEM((4,), jnp.int32),
            pltpu.SMEM((1, 2), F32),
            pltpu.VMEM((8, 512), BF16),
            pltpu.VMEM((512,), F32),
            pltpu.VMEM((2, 24, 64, 128), BF16),
            pltpu.VMEM((1024, 512), BF16),
            pltpu.VMEM((2, 2, 512, 768), BF16),
            pltpu.VMEM((2, 768, 512), BF16),
            pltpu.VMEM((32, 128), F32),
            pltpu.VMEM((2, 8, 128), F32),
            pltpu.VMEM((16, 32, 128), BF16),
            pltpu.VMEM((8, 16, 256), BF16),
            pltpu.VMEM((8, 16, 256), BF16),
            pltpu.VMEM((8, 512), F32),
            pltpu.VMEM((16, 16, 256), BF16),
            pltpu.VMEM((2, 16, 16, 768), BF16),
            pltpu.VMEM((2, 16, 16, 768), BF16),
            pltpu.VMEM((8, 128), F32),
            pltpu.VMEM((16, 8, 128), F32),
            pltpu.VMEM((8, 128), F32),
            pltpu.VMEM((2, 8, 128), F32),
            pltpu.VMEM((2, 2, 8, 16, 384), BF16),
            pltpu.VMEM((16, 16, 256), BF16),
            pltpu.VMEM((16, 16, 256), BF16),
            sems((11,)), sems((4,)), sems((2,)), sems((2,)), sems((16,)), sems((3,)), sems((2,)),
            sems((3,)), sems((3,)), sems((2,)),
        ],
        compiler_params=pltpu.CompilerParams(
            collective_id=0, has_side_effects=True, vmem_limit_bytes=64 << 20
        ),
        name="decode_layer",
    )(
        queries, fresh_kv, key_value_pages, page_table, lengths, cache_scales.T, residual,
        out_weight, norm_gain, gate_up, down_weight,
    )


def solution(mesh):
    placed = (
        P(("pool", "dp"), "head"),
        P(None, ("pool", "dp"), "head"),
        P(None, ("pool", "dp"), None, "head"),
        P(("pool", "dp"), None),
        P(("pool", "dp")),
        P(None, "head"),
        P(("pool", "head"), "dp"),
        P("head", "dp"),
        P("dp"),
        P(None, "dp", ("pool", "head")),
        P(("pool", "head"), "dp"),
    )
    return jax.shard_map(
        body, mesh=mesh, in_specs=placed, out_specs=P(("pool", "head"), "dp"), check_vma=False
    )
```

```python
import math

import jax
import jax.numpy as jnp
from jax import lax
from jax.experimental import pallas as pl
from jax.experimental.pallas import tpu as pltpu
from jax.sharding import PartitionSpec as P

D = 8192
HEAD_DIM = 128
MESH = pl.DeviceIdType.MESH
OFFSETS = (0, 1, -1, 2, -2, 3, -3, 4, -4, 5, -5, 6, -6, 7, -7, 8)
SLOT = {o % 16: i for i, o in enumerate(OFFSETS)}
GROUPS = ((0, 3), (3, 8), (8, 16))
ALONG_Z = (1, -1, 8, 7, -7, 6, -6, 5, -5, 4, -4, 3, -3, 2, -2)
NEAR = ((0, 1), (0, 3), (1, 0), (3, 0))
MIDDLE = ((0, 2), (2, 0), (1, 1), (1, 3), (3, 1), (3, 3))
FAR = ((1, 2), (2, 1), (3, 2), (2, 3), (2, 2))
F32 = jnp.float32
BF16 = jnp.bfloat16


def place():
    pool, dp, head = (lax.axis_index(name) for name in ("pool", "dp", "head"))
    return (pool // 2) * 8 + head, pool % 2, dp // 4, dp % 4


def device(z, core, y, x):
    return ((z // 8) * 2 + core, y * 4 + x, z % 8)


def send(src, dst, send_sem, recv_sem, to):
    pltpu.make_async_remote_copy(
        src_ref=src, dst_ref=dst, send_sem=send_sem, recv_sem=recv_sem,
        device_id=to, device_id_type=MESH,
    ).start()


def wait(ref, sem):
    pltpu.make_async_copy(ref, ref, sem).wait()


def to_tile(v):
    return jnp.concatenate([v[..., :256], v[..., 256:]], axis=-2).astype(BF16)


def from_tile(v):
    v = v.astype(F32)
    return jnp.concatenate([v[..., :8, :], v[..., 8:, :]], axis=-1)


def attend(q_ref, fresh_ref, kv, table, lengths, scales, q_rows, fresh_rows):
    q = q_ref[...].astype(F32)
    for g in range(8):
        q_rows[g * 4 : g * 4 + 4, :] = q[:, g * 128 : (g + 1) * 128]
    fresh = fresh_ref[...].astype(F32)
    for i in range(2):
        fresh_rows[i, 0:4, :] = fresh[i]
        fresh_rows[i, 4:8, :] = fresh[i]
    asked = q_rows[...]
    row = lax.broadcasted_iota(jnp.int32, (8, 1), 0) & 3
    column = lax.broadcasted_iota(jnp.int32, (8, 1536), 1)
    page, line = column >> 6, column & 63

    def by_request(values):
        a, b, c, d = values
        return jnp.where(row == 0, a, jnp.where(row == 1, b, jnp.where(row == 2, c, d)))

    length = by_request([lengths[t] for t in range(4)])
    live = jnp.zeros((8, 1536), jnp.bool_)
    for j in range(8):
        entry = by_request([table[t, j] for t in range(4)])
        live = live | ((page == entry) & (line < length - 64 * j))
    factor = 1.0 / math.sqrt(HEAD_DIM)
    keys = kv[0].reshape(1536, 128)
    scores = lax.dot_general(
        asked.astype(BF16), keys, (((1,), (1,)), ((), ())), preferred_element_type=F32
    ) * (scales[0, 0] * factor)
    scores = jnp.where(live[None], scores.reshape(4, 8, 1536), -jnp.inf)
    own = jnp.sum(asked.reshape(4, 8, 128) * fresh_rows[0][None], axis=2, keepdims=True) * factor
    top = jnp.maximum(jnp.max(scores, axis=2, keepdims=True), own)
    e = jnp.exp(scores - top)
    e_own = jnp.exp(own - top)
    total = jnp.sum(e, axis=2, keepdims=True) + e_own
    probs = (e / total).astype(BF16)
    own_prob = (e_own / total).astype(BF16).astype(F32)
    mixed = jnp.dot(
        probs.reshape(32, 1536), kv[1].reshape(1536, 128), preferred_element_type=F32
    ) * scales[0, 1]
    mixed = mixed.reshape(4, 8, 128) + own_prob * fresh_rows[1][None]
    return mixed.reshape(32, 128).astype(BF16)


def kernel(
    q_hbm, fresh_hbm, pages_hbm, table_hbm, lengths_hbm, scales_hbm, residual_hbm, out_w_hbm,
    gain_hbm, gate_up_hbm, down_hbm, out_ref,
    q_ref, fresh_ref, table, lengths, scales, residual_ref, gain_ref, kv, out_w, gate_up, down, q_rows, fresh_rows, att, b_send, b_recv, stream, normed,
    d_send, d_recv, sq_send, sq_recv, scale_send, scale_recv, hidden,
    g_send, g_recv,
    load_sem, pair_sem, a_sem, b_sem, c_sem, d_sem, sq_sem, scale_sem,
    h_sem, g_sem,
):
    z, core, y, x = place()
    dp = y * 4 + x
    head = z % 8

    pairs = (
        (table_hbm, table), (lengths_hbm, lengths), (scales_hbm, scales), (q_hbm, q_ref),
        (fresh_hbm, fresh_ref), (pages_hbm, kv), (residual_hbm, residual_ref), (gain_hbm, gain_ref),
        (out_w_hbm, out_w), (gate_up_hbm, gate_up.at[core]), (down_hbm, down.at[core]),
    )
    loads = [
        pltpu.make_async_copy(src, dst, load_sem.at[i]) for i, (src, dst) in enumerate(pairs)
    ]
    for load in loads:
        load.start()

    def plane(dy, dx):
        return device(z, core, (y + dy) % 4, (x + dx) % 4)

    def ring(k):
        return device((z + k + 16) % 16, core, y, x)

    sibling = device(z, 1 - core, y, x)
    others = FAR[::-1] + MIDDLE + NEAR

    barrier = pltpu.get_barrier_semaphore()

    def greet(to):
        pl.semaphore_signal(barrier, inc=1, device_id=to, device_id_type=MESH)

    for k in sorted(ALONG_Z, key=abs, reverse=True):
        greet(ring(k))
    for step in others:
        greet(plane(*step))
    greet(sibling)

    for load in loads[:6]:
        load.wait()
    att[dp] = attend(q_ref, fresh_ref, kv, table, lengths, scales, q_rows, fresh_rows)
    pl.semaphore_wait(barrier, 31)
    for step in others:
        send(att.at[dp], att.at[dp], a_sem.at[0], a_sem.at[1], plane(*step))
    send(gate_up_hbm, gate_up.at[core], pair_sem.at[0], pair_sem.at[1], sibling)
    for load in loads[6:9]:
        load.wait()
    wait(att.at[0:15], a_sem.at[1])

    rows = att[...].astype(F32).reshape(8, 2, 4, 8, 128)
    even, odd = rows[:, 0], rows[:, 1]
    upper = lax.broadcasted_iota(jnp.int32, (8, 128), 0) < 4

    def swap(v):
        return pltpu.roll(v.reshape(32 * 8, 128).reshape(32, 8, 128), 4, 1).reshape(8, 4, 8, 128)

    low = jnp.where(upper, even, swap(odd))
    high = jnp.where(upper, swap(even), odd)
    columns = []
    for g in range(8):
        columns.append((low if g % 2 == 0 else high)[:, g // 2].reshape(64, 128))
    attended = jnp.concatenate(columns, axis=1).astype(BF16)
    projected = jnp.dot(attended, out_w[...], preferred_element_type=F32)
    b_send[...] = to_tile(projected.reshape(8, 8, 512))
    for i in range(7):
        up_to, down_to = 7 - i, i
        up_to = up_to - jnp.where(up_to <= head, 1, 0)
        down_to = down_to + jnp.where(down_to >= head, 1, 0)
        to = jnp.where(head < 4, up_to, down_to)
        send(b_send.at[to], b_recv.at[head], b_sem.at[0], b_sem.at[1], device((z // 8) * 8 + to, core, y, x))
    b_recv[head] = b_send[head]
    send(down_hbm, down.at[core], pair_sem.at[2], pair_sem.at[3], sibling)
    wait(b_recv.at[0:7], b_sem.at[1])
    summed = from_tile(jnp.sum(b_recv[...].astype(F32), axis=0))
    stream[...] = residual_ref[...].astype(F32) + summed

    gain = gain_ref[...].reshape(1, 512)
    normed[0] = to_tile(stream[...] * gain)
    for k in ALONG_Z:
        slot = SLOT[-k % 16]
        send(normed.at[0], normed.at[slot], c_sem.at[0], c_sem.at[slot], ring(k))

    squares = stream[...] * stream[...]
    sq_send[...] = squares[:, :128] + squares[:, 128:256] + squares[:, 256:384] + squares[:, 384:]
    for step in others:
        send(sq_send, sq_recv.at[dp], sq_sem.at[0], sq_sem.at[1], plane(*step))
    sq_recv[dp] = sq_send[...]

    unit = ((x - y + 4) % 4) * 4 + y
    unit_chip, unit_core = unit // 2, unit % 2

    def unit_ring(phase):
        slot = 8 * phase + unit_chip
        return ((slot + 1) // 2) * (2 * (slot % 2) - 1)

    def scales_out():
        wait(sq_recv.at[0:15], sq_sem.at[1])
        mean = jnp.sum(jnp.sum(sq_recv[...], axis=0), axis=1, keepdims=True) / D
        scale_send[...] = jnp.broadcast_to(lax.rsqrt(mean + 1e-6), (8, 128))
        send(scale_send, scale_recv.at[1], scale_sem.at[0], scale_sem.at[2], ring(-unit_ring(1)))

        @pl.when(unit_chip != 0)
        def _():
            send(scale_send, scale_recv.at[0], scale_sem.at[0], scale_sem.at[1], ring(-unit_ring(0)))

        @pl.when(unit_chip == 0)
        def _():
            scale_recv[0] = scale_send[...]

    def feed(group):
        lo, hi = GROUPS[group]
        n = hi - lo
        for slot in range(max(lo, 1), hi):
            wait(normed.at[0], c_sem.at[slot])
        lhs = from_tile(normed[lo:hi]).reshape(8 * n, 512).astype(BF16)
        for c in range(2):
            gate = jnp.dot(lhs, gate_up[c, 0], preferred_element_type=F32).reshape(n, 8, 768)
            up = jnp.dot(lhs, gate_up[c, 1], preferred_element_type=F32).reshape(n, 8, 768)
            d_send[c, lo:hi] = jnp.concatenate([gate, up], axis=1).astype(BF16)
            for slot in range(lo, hi):
                phase, u = slot // 8, 2 * (slot % 8) + c
                oy, ox = u % 4, (u % 4 + u // 4) % 4
                same = dp == oy * 4 + ox

                @pl.when(jnp.logical_not(same))
                def _():
                    send(
                        d_send.at[c, slot], d_recv.at[phase, dp], d_sem.at[0], d_sem.at[1 + phase],
                        device(z, core, oy, ox),
                    )

                @pl.when(same)
                def _():
                    d_recv[phase, dp] = d_send[c, slot]

    def share_hidden(phase):
        if phase == 0:

            @pl.when(unit_chip != 0)
            def _():
                wait(scale_send, scale_sem.at[1])
        else:
            wait(scale_send, scale_sem.at[2])
        scale = scale_recv[phase][:, :1]
        wait(d_recv.at[0, 0:15], d_sem.at[1 + phase])
        total = d_recv[phase, 0].astype(F32)
        for i in range(1, 16):
            total = total + d_recv[phase, i].astype(F32)
        gate, up = total[:8] * scale, total[8:] * scale
        own = gate / (1.0 + jnp.exp(-gate)) * up
        hidden[phase, unit_core, unit_chip] = jnp.concatenate([own[:, :384], own[:, 384:]], axis=0).astype(BF16)
        mine = hidden.at[phase, unit_core, unit_chip]
        for step in others:
            send(mine, mine, h_sem.at[0], h_sem.at[1 + phase], plane(*step))

    def lower(phase):
        wait(d_recv.at[0, 0:15, :, 0:384], h_sem.at[1 + phase])
        lowered = jnp.zeros((64, 512), F32)
        for c in range(2):
            tokens = hidden[phase, c].astype(F32)
            lhs = jnp.concatenate([tokens[:, :8], tokens[:, 8:]], axis=2).reshape(64, 768).astype(BF16)
            lowered = lowered + jnp.dot(lhs, down[c], preferred_element_type=F32)
        g_send[8 * phase : 8 * phase + 8] = to_tile(lowered.reshape(8, 8, 512))
        for slot in range(8 * phase + 7, 8 * phase - 1, -1):
            if slot == 0:
                g_recv[0] = g_send[0]
            else:
                send(g_send.at[slot], g_recv.at[slot], g_sem.at[0], g_sem.at[1], ring(OFFSETS[slot]))

    loads[9].wait()
    wait(gate_up.at[0], pair_sem.at[1])
    feed(0)
    feed(1)
    scales_out()
    feed(2)
    share_hidden(0)
    share_hidden(1)
    loads[10].wait()
    wait(down.at[0], pair_sem.at[3])
    lower(0)
    lower(1)
    wait(g_recv.at[1:16], g_sem.at[1])
    lowered = from_tile(jnp.sum(g_recv[...].astype(F32), axis=0))
    out_ref[...] = (stream[...] + lowered).astype(BF16)

    wait(gate_up.at[0], pair_sem.at[0])
    wait(down.at[0], pair_sem.at[2])
    wait(att.at[0:15], a_sem.at[0])
    wait(b_recv.at[0:7], b_sem.at[0])
    wait(normed.at[0:15], c_sem.at[0])
    wait(d_recv.at[:, 0:15], d_sem.at[0])
    wait(sq_recv.at[0:15], sq_sem.at[0])
    wait(scale_send, scale_sem.at[0])

    @pl.when(unit_chip != 0)
    def _():
        wait(scale_send, scale_sem.at[0])

    wait(d_recv.at[0, 0:15], h_sem.at[0])
    wait(g_recv.at[0:15], g_sem.at[0])


def body(
    queries, fresh_kv, key_value_pages, page_table, lengths, cache_scales, residual, out_weight,
    norm_gain, gate_up, down_weight,
):
    vmem = pl.BlockSpec(memory_space=pltpu.VMEM)
    anywhere = pl.BlockSpec(memory_space=pl.ANY)
    sems = pltpu.SemaphoreType.DMA
    return pl.pallas_call(
        kernel,
        out_shape=jax.ShapeDtypeStruct((8, 512), BF16),
        in_specs=[anywhere] * 11,
        out_specs=vmem,
        scratch_shapes=[
            pltpu.VMEM((4, 1024), BF16),
            pltpu.VMEM((2, 4, 128), BF16),
            pltpu.SMEM((4, 8), jnp.int32),
            pltpu.SMEM((4,), jnp.int32),
            pltpu.SMEM((1, 2), F32),
            pltpu.VMEM((8, 512), BF16),
            pltpu.VMEM((512,), F32),
            pltpu.VMEM((2, 24, 64, 128), BF16),
            pltpu.VMEM((1024, 512), BF16),
            pltpu.VMEM((2, 2, 512, 768), BF16),
            pltpu.VMEM((2, 768, 512), BF16),
            pltpu.VMEM((32, 128), F32),
            pltpu.VMEM((2, 8, 128), F32),
            pltpu.VMEM((16, 32, 128), BF16),
            pltpu.VMEM((8, 16, 256), BF16),
            pltpu.VMEM((8, 16, 256), BF16),
            pltpu.VMEM((8, 512), F32),
            pltpu.VMEM((16, 16, 256), BF16),
            pltpu.VMEM((2, 16, 16, 768), BF16),
            pltpu.VMEM((2, 16, 16, 768), BF16),
            pltpu.VMEM((8, 128), F32),
            pltpu.VMEM((16, 8, 128), F32),
            pltpu.VMEM((8, 128), F32),
            pltpu.VMEM((2, 8, 128), F32),
            pltpu.VMEM((2, 2, 8, 16, 384), BF16),
            pltpu.VMEM((16, 16, 256), BF16),
            pltpu.VMEM((16, 16, 256), BF16),
            sems((11,)), sems((4,)), sems((2,)), sems((2,)), sems((16,)), sems((3,)), sems((2,)),
            sems((3,)), sems((3,)), sems((2,)),
        ],
        compiler_params=pltpu.CompilerParams(
            collective_id=0, has_side_effects=True, vmem_limit_bytes=64 << 20
        ),
        name="decode_layer",
    )(
        queries, fresh_kv, key_value_pages, page_table, lengths, cache_scales.T, residual,
        out_weight, norm_gain, gate_up, down_weight,
    )


def solution(mesh):
    placed = (
        P(("pool", "dp"), "head"),
        P(None, ("pool", "dp"), "head"),
        P(None, ("pool", "dp"), None, "head"),
        P(("pool", "dp"), None),
        P(("pool", "dp")),
        P(None, "head"),
        P(("pool", "head"), "dp"),
        P("head", "dp"),
        P("dp"),
        P(None, "dp", ("pool", "head")),
        P(("pool", "head"), "dp"),
    )
    return jax.shard_map(
        body, mesh=mesh, in_specs=placed, out_specs=P(("pool", "head"), "dp"), check_vma=False
    )
```
